128 devices in a mesh: dp: 4 (over x), section: 4 (over y_hi, core), expert: 8 (over y_lo, z).
Axes of the slice: x: 4, y: 4 (y_hi: 2, y_lo: 2; y = y_hi * 2 + y_lo), z: 4, core: 2. Of those that a mesh axis runs over, the one named last changes fastest.
Arguments:
- tokens: bfloat16 [8192, 4096], P(('dp', 'section')), may hold values from -90 to 90
- w_query: bfloat16 [4096, 2048], P(None, 'expert'), may hold values from -0.09375 to 0.09375
- w_key: bfloat16 [4096, 1024], P(None, 'expert'), may hold values from -0.09375 to 0.09375
- w_value: bfloat16 [4096, 1024], P(None, 'expert'), may hold values from -0.09375 to 0.09375
- w_out: bfloat16 [2048, 4096], P('expert'), may hold values from -0.125 to 0.125
- w_gate: bfloat16 [8, 7168, 4096], P('expert', ('dp', 'section')), may hold values from -0.09375 to 0.09375
- w_up: bfloat16 [8, 7168, 4096], P('expert', ('dp', 'section')), may hold values from -0.09375 to 0.09375
- w_down: bfloat16 [8, 7168, 4096], P('expert', ('dp', 'section')), may hold values from -0.0625 to 0.0625
- route: int32 [128, 1], P(('dp', 'section')), may hold values from 0 to 7; in each aligned block of 8 rows (0 to 7, 8 to 15, ...) at most 2 rows name the same one
- old_out: bfloat16 [128, 64, 4096], P(('dp', 'section'), 'expert'), may hold values from -6 to 6
- cotangent: bfloat16 [8192, 4096], P(('dp', 'section')), may hold values from -6 to 6
Outputs:
- joined: bfloat16 [128, 64, 4096], P(('dp', 'section'), 'expert')
- divergence: float32 [128, 64], P(('dp', 'section'), 'expert')
- grad_out_t: float32 [4096, 2048], P(('dp', 'section'), 'expert')
The draws below stay inside these ranges and needn't reach their ends.
Inputs may be any that keep to these rules, and one draw needn't show every extreme that they name: `route`: blocks routed to experts 6 and above go to new experts. Among the 8 blocks of one replica no expert is named more than 2 times, and some replica names one expert exactly 2 times in every draw.
All inputs are finite; a program needn't handle non-finite values.
Results may differ from the reference program's by a relative error of at most 0.025.
Values may be sent and summed in bfloat16 or wider, within the bound.
No kernel may reach another device: no remote copies, remote signals or barrier semaphores. Data moves between devices by JAX's collectives and lax.ppermute only.
A program may use at most 192 MiB of HBM per device.

```python
import math
import jax
import jax.numpy as jnp
import numpy as np
from jax import lax

D = 4096
HEADS = 16
KV_HEADS = 8
HEAD_DIM = 128
FFW = 7168
BLOCK = 64
SEQ = 512
EXPERTS = 8
OLD = 6
NB = 8
NBT = 128
TOKENS = 8192
CAP = 2
N_DP = 4
N_SECTION = 4


def draw_tokens(key, part):
    noise = jax.random.truncated_normal(jax.random.fold_in(key, 11), -6.0, 6.0, (TOKENS, D), jnp.float32)
    return noise.astype(jnp.bfloat16)


def strengthened(values, stream_key, source, target, blocks, factor):
    def block_of(axis_at):
        return (jnp.arange(values.shape[axis_at]) // (values.shape[axis_at] // blocks)).reshape((-1,) + (1,) * (values.ndim - 1 - axis_at))

    one_side = jax.random.permutation(stream_key, blocks)[block_of(target)]
    other_side = (block_of(target) + blocks // 2) % blocks
    return jnp.where((block_of(source) == one_side) | (block_of(source) == other_side), factor * values, values)


def levels(stream_key, shape, shards, low, largest):
    gain, own = 1.0, jax.random.fold_in(stream_key, 6)
    for position, shards_of in shards:
        heights = jnp.exp(jax.random.uniform(jax.random.fold_in(own, position), (shards_of,), jnp.float32, low / len(shards), largest / len(shards)))
        gain = gain * jnp.repeat(heights, shape[position] // shards_of).reshape([-1 if axis == position else 1 for axis in range(len(shape))])
    return gain


def deal_out(key, own, number, rows, count, top, reach, lean):
    order = jax.random.permutation(key, count)
    packed, ordinary = portions_of(count, rows * top, reach, lean, True), portions_of(count, rows * top, reach, lean, False)
    places = jnp.arange(count)

    def named(lengths, turn):
        used = int((lengths > 0).sum())
        fixed = max(1, used // 4)
        passed = fixed + (places - fixed + turn * (used - fixed)) % max(1, count - fixed)
        return jnp.zeros((count,), jnp.int32).at[order[jnp.where(places < fixed, places, passed)]].set(jnp.asarray(lengths, jnp.int32))

    lengths = jnp.where(number % 4 == 0, named(packed, number // 4), named(ordinary, number - number // 4 - 1))
    mixed = jax.random.permutation(jax.random.fold_in(own, 3), count)
    source_of, taker = mixed[0:count // 2 * 2:2], mixed[1:count // 2 * 2:2]
    margin = jnp.minimum(lengths[source_of] - 1, reach - lengths[taker]) // 2
    margin = jnp.where((source_of == order[0]) | (taker == order[0]) | (lengths[taker] == 0), 0, jnp.maximum(margin, 0))
    passed = jax.random.randint(jax.random.fold_in(own, 4), (count // 2,), 0, 1 << 20) % (margin + 1)
    lengths = lengths.at[source_of].add(-passed).at[taker].add(passed)
    items = jnp.searchsorted(jnp.cumsum(lengths), jnp.arange(rows * top), side="right").astype(jnp.int32)
    listing = items.reshape(top, rows).T
    listing = listing[jax.random.permutation(jax.random.fold_in(own, 1), rows)]
    turn = jax.random.randint(jax.random.fold_in(own, 2), (rows, 1), 0, top)
    return jnp.take_along_axis(listing, (jnp.arange(top)[None, :] + turn) % top, axis=1)


def portions_of(amount, total, reach, lean, full):
    weights = [(1 << 20) // math.isqrt(grade ** lean) + 1 for grade in range(1, amount + 1)]
    largest = reach if full else min(reach, max(-(-total // amount), total * weights[0] // sum(weights)))
    least = 1 if total - largest >= amount - 1 else 0
    given, rest = [largest] + [least] * (amount - 1), total - largest - least * (amount - 1)
    while rest > 0:
        movable = [i for i in range(1, amount) if given[i] < largest] or [i for i in range(1, amount) if given[i] < reach]
        whole, left = sum([weights[i] for i in movable]), rest
        for i in movable:
            extra = min(reach - given[i], max(1, left * weights[i] // whole), rest)
            given[i] = given[i] + extra
            rest = rest - extra
    return np.array(given)


def gaussian(own_key, shape, deviation, limit, cuts=(), held_as=jnp.bfloat16):
    array = deviation * jax.random.normal(own_key, shape, jnp.float32)
    if cuts:
        array = array * levels(own_key, shape, cuts, -0.22, 0.18)
    return jnp.clip(array, -limit, limit).astype(held_as)


def bell_draw_with(key, extent, spread, reach, split, heavy, dtype=jnp.bfloat16):
    entries = spread * jax.random.normal(key, extent, jnp.float32)
    if split:
        entries = entries * levels(key, extent, split, -0.22, 0.18)
    return jnp.clip(strengthened(entries, jax.random.fold_in(key, 3), *heavy), -reach, reach).astype(dtype)


def setup_inputs(seed: int = 0) -> dict:
    splits = jax.random.split(jax.random.key(seed), 12)
    tokens = draw_tokens(jax.random.fold_in(splits[11], 71), 0)
    w_query = gaussian(splits[1], (D, HEADS * HEAD_DIM), D ** -0.5, 0.09375, ((1, 8),))
    w_key = gaussian(splits[2], (D, KV_HEADS * HEAD_DIM), D ** -0.5, 0.09375, ((1, 8),))
    w_value = gaussian(splits[3], (D, KV_HEADS * HEAD_DIM), D ** -0.5, 0.09375, ((1, 8),))
    w_out = gaussian(splits[4], (HEADS * HEAD_DIM, D), (HEADS * HEAD_DIM) ** -0.5, 0.125, ((0, 8),))
    w_gate = gaussian(splits[5], (EXPERTS, FFW, D), D ** -0.5, 0.09375, ((0, 8), (1, 16)))
    w_up = gaussian(splits[6], (EXPERTS, FFW, D), D ** -0.5, 0.09375, ((0, 8), (1, 16)))
    w_down = gaussian(splits[7], (EXPERTS, FFW, D), FFW ** -0.5, 0.0625, ((0, 8), (1, 16)))
    route_keys = jax.random.split(jax.random.fold_in(splits[8], 1), NBT // NB)
    route_turns = jax.random.permutation(jax.random.fold_in(splits[8], 3), NBT // NB)
    route = jax.vmap(lambda own, number: deal_out(jax.random.fold_in(splits[8], 2), own, number, NB, EXPERTS, 1, CAP, 2))(route_keys, route_turns).reshape((NBT, 1))
    old_out = gaussian(splits[9], (NBT, BLOCK, D), 1.0, 6.0, ((0, 16), (1, 8)))
    cotangent = bell_draw_with(splits[10], (TOKENS, D), 1.0, 6.0, ((0, 16),), (0, 1, 16, 2.0))
    return {"tokens": tokens, "w_query": w_query, "w_key": w_key, "w_value": w_value, "w_out": w_out, "w_gate": w_gate, "w_up": w_up, "w_down": w_down, "route": route, "old_out": old_out, "cotangent": cotangent}


def attend_all(sequence, w_query, w_key, w_value):
    length = sequence.shape[0]
    group = HEADS // KV_HEADS
    queries = jnp.dot(sequence, w_query, preferred_element_type=jnp.float32).astype(jnp.bfloat16)
    keys = jnp.dot(sequence, w_key, preferred_element_type=jnp.float32).astype(jnp.bfloat16)
    values = jnp.dot(sequence, w_value, preferred_element_type=jnp.float32).astype(jnp.bfloat16)
    queries = queries.astype(jnp.float32).reshape(length, KV_HEADS, group, HEAD_DIM)
    keys = keys.astype(jnp.float32).reshape(length, KV_HEADS, HEAD_DIM)
    values = values.astype(jnp.float32).reshape(length, KV_HEADS, HEAD_DIM)
    scores = jnp.einsum('qkgd,skd->kgqs', queries, keys) * (1.0 / math.sqrt(HEAD_DIM))
    causal = jnp.arange(length)[:, None] >= jnp.arange(length)[None, :]
    scores = jnp.where(causal, scores, -jnp.inf)
    top = lax.optimization_barrier(jnp.max(scores, axis=-1, keepdims=True))
    weights = jnp.exp(scores - top)
    probs = (weights / lax.optimization_barrier(jnp.sum(weights, axis=-1, keepdims=True))).astype(jnp.bfloat16)
    mixed = jnp.einsum('kgqs,skd->qkgd', probs.astype(jnp.float32), values)
    return mixed.reshape(length, HEADS * HEAD_DIM).astype(jnp.bfloat16)

def expert_block(block_rows, expert, w_gate, w_up, w_down):
    slices = N_DP * N_SECTION
    width = FFW // slices
    gate_rows = lax.dynamic_index_in_dim(w_gate, expert, 0, keepdims=False)
    up_rows = lax.dynamic_index_in_dim(w_up, expert, 0, keepdims=False)
    down_rows = lax.dynamic_index_in_dim(w_down, expert, 0, keepdims=False)
    contract = (((1,), (1,)), ((), ()))
    gate = lax.dot_general(block_rows, gate_rows, contract, preferred_element_type=jnp.float32)
    lifted = lax.dot_general(block_rows, up_rows, contract, preferred_element_type=jnp.float32)
    active = (jax.nn.silu(gate) * lifted).astype(jnp.bfloat16)
    active = active.astype(jnp.float32).reshape(BLOCK, slices, width)
    down = down_rows.astype(jnp.float32).reshape(slices, width, D)
    partial_value = jnp.einsum('tsh,shd->std', active, down)
    partial_value = lax.optimization_barrier(partial_value.astype(jnp.bfloat16)).astype(jnp.float32)
    return lax.optimization_barrier(jnp.sum(partial_value, axis=0)).astype(jnp.bfloat16)

def reference(tokens, w_query, w_key, w_value, w_out, w_gate, w_up, w_down, route, old_out, cotangent):
    replicas = N_DP * N_SECTION
    sequences = tokens.reshape(replicas, SEQ, D)
    routes = route.reshape(replicas, NB)
    olds = old_out.reshape(replicas, NB, BLOCK, D)
    cotangents = cotangent.reshape(replicas, SEQ, D)

    def one_replica(total, item):
        sequence, seq_routes, seq_old, seq_cot = item
        heads_out = attend_all(sequence, w_query, w_key, w_value)
        attention = jnp.dot(heads_out, w_out, preferred_element_type=jnp.float32)
        hidden_in = (sequence.astype(jnp.float32) + attention).astype(jnp.bfloat16)
        blocks_in = hidden_in.reshape(NB, BLOCK, D)
        expert_out = lax.map(lambda pair: expert_block(pair[0], pair[1], w_gate, w_up, w_down), (blocks_in, seq_routes))
        joined = (blocks_in.astype(jnp.float32) + expert_out.astype(jnp.float32)).astype(jnp.bfloat16)
        gap = joined.astype(jnp.float32) - seq_old.astype(jnp.float32)
        fresh = (seq_routes >= OLD).astype(jnp.float32)
        divergence = 0.5 * lax.optimization_barrier(jnp.mean(gap * gap, axis=-1)) * fresh[:, None]
        term = jnp.dot(seq_cot.T, heads_out, preferred_element_type=jnp.float32)
        term = lax.optimization_barrier(term.astype(jnp.bfloat16)).astype(jnp.float32)
        return (total + term, (joined, divergence))
    start = jnp.zeros((D, HEADS * HEAD_DIM), jnp.float32)
    grad, (joined, divergence) = lax.scan(one_replica, start, (sequences, routes, olds, cotangents))
    return (joined.reshape(NBT, BLOCK, D), divergence.reshape(NBT, BLOCK), grad)
```

```python
import functools
import math

import jax
import jax.numpy as jnp
from jax import lax
from jax.experimental import pallas as pl
from jax.experimental.pallas import tpu as pltpu
from jax.sharding import Mesh
from jax.sharding import PartitionSpec as P

D = 4096
HEAD_DIM = 128
BLOCK = 64
SIZES = {"x": 4, "yh": 2, "core": 2, "yl": 2, "z": 4}
AXES = ("x", "yh", "core", "yl", "z")
BF = jnp.bfloat16
F32 = jnp.float32


def shift(value, axis, by):
    n = SIZES[axis]
    return lax.ppermute(value, axis, [(i, (i + by) % n) for i in range(n)])


def rows_of(*parts):
    return jnp.concatenate(parts, axis=0)


def plus(first, *others):
    total = first.astype(F32)
    for other in others:
        total = total + other.astype(F32)
    return total.astype(BF)


def attend_local(tokens, w_query, w_key, w_value):
    length = tokens.shape[0]
    group = w_query.shape[1] // w_key.shape[1]
    queries = jnp.dot(tokens, w_query, preferred_element_type=F32).astype(BF)
    queries = queries.reshape(length, group, HEAD_DIM)
    keys = jnp.dot(tokens, w_key, preferred_element_type=F32).astype(BF)
    values = jnp.dot(tokens, w_value, preferred_element_type=F32).astype(BF)
    scores = jnp.einsum("qgd,sd->gqs", queries, keys, preferred_element_type=F32)
    scores = scores * (1.0 / math.sqrt(HEAD_DIM))
    query_pos = lax.broadcasted_iota(jnp.int32, (length, length), 0)
    key_pos = lax.broadcasted_iota(jnp.int32, (length, length), 1)
    scores = jnp.where(query_pos >= key_pos, scores, -jnp.inf)
    top = jnp.max(scores, axis=-1, keepdims=True)
    weights = jnp.exp(scores - top)
    probs = (weights / jnp.sum(weights, axis=-1, keepdims=True)).astype(BF)
    mixed = jnp.einsum("gqs,sd->qgd", probs, values, preferred_element_type=F32)
    return mixed.astype(BF).reshape(length, group * HEAD_DIM)


def routing_table(routes, experts, capacity):
    number = routes.shape[0]
    same = routes[:, None] == routes[None, :]
    earlier = lax.broadcasted_iota(jnp.int32, (number, number), 1) < lax.broadcasted_iota(
        jnp.int32, (number, number), 0
    )
    slot = jnp.sum((same & earlier).astype(jnp.int32), axis=1)
    expert_hit = routes[None, :] == lax.broadcasted_iota(jnp.int32, (experts, number), 0)
    slot_hit = slot[None, :] == lax.broadcasted_iota(jnp.int32, (capacity, number), 0)
    return expert_hit[:, None, :] & slot_hit[None, :, :]


def gather_start(first, second, ring, pair):
    return shift(first, pair, 1), shift(second, ring, 1), shift(second, ring, -1)


def gather_middle(first, second, arrived):
    first_p, second_l, second_r = arrived
    half = second.shape[0] // 2
    return (
        rows_of(first, first_p, second_l[:half]),
        rows_of(first, first_p, second_r[half:]),
        rows_of(second, second_l, second_r),
    )


def gather_send(payload, ring, pair):
    return shift(payload[0], ring, 1), shift(payload[1], ring, -1), shift(payload[2], pair, 1)


def gather_last(arrived, n):
    left, right, _ = arrived
    return left[:n], right[n : 2 * n], rows_of(left[2 * n :], right[2 * n :])


def project_kernel(number, *refs):
    lhs, weights, out = refs[:number], refs[number : 2 * number], refs[2 * number]
    total = jnp.zeros(out.shape, F32)
    for left, right in zip(lhs, weights):
        total = total + jnp.dot(left[...], right[...], preferred_element_type=F32)
    out[...] = total.astype(BF)


def project(lhs, weights):
    rows, width = lhs[0].shape[0], weights[0].shape[1]
    tile = 512
    number = len(lhs)
    depth = sum(w.shape[0] for w in weights)
    return pl.pallas_call(
        functools.partial(project_kernel, number),
        grid=(width // tile,),
        in_specs=[pl.BlockSpec(v.shape, lambda j: (0, 0)) for v in lhs]
        + [pl.BlockSpec((w.shape[0], tile), lambda j: (0, j)) for w in weights],
        out_specs=pl.BlockSpec((rows, tile), lambda j: (0, j)),
        out_shape=jax.ShapeDtypeStruct((rows, width), BF),
        compiler_params=pltpu.CompilerParams(vmem_limit_bytes=32 * 1024 * 1024),
        cost_estimate=pl.CostEstimate(
            flops=2 * rows * width * depth, bytes_accessed=2 * depth * (rows + width), transcendentals=0
        ),
    )(*lhs, *weights)


OUT_TILES = 4
HIDDEN_TILE = 256


def ffn_kernel(rows, *refs):
    number = len(rows)
    pieces = refs[:number]
    gates, ups, downs = refs[number : number + 2], refs[number + 2 : number + 4], refs[number + 4 : number + 6]
    outs = refs[number + 6 : 2 * number + 6]
    x, wg, wu, wd, act, res, x_sem, g_sem, u_sem, d_sem, o_sem = refs[2 * number + 6 :]
    hidden = gates[0].shape[0]

    x_copies, out_copies = [], []
    start = 0
    for i, count in enumerate(rows):
        part = pl.ds(start, count)
        x_copies.append(pltpu.make_async_copy(pieces[i], x.at[part], x_sem.at[i]))
        out_copies.append(pltpu.make_async_copy(res.at[part], outs[i], o_sem.at[i]))
        start += count
    g_copies, u_copies, d_copies = [], [], []
    for side in range(2):
        part = pl.ds(side * hidden, hidden)
        g_copies.append(pltpu.make_async_copy(gates[side], wg.at[part], g_sem.at[side]))
        u_copies.append(pltpu.make_async_copy(ups[side], wu.at[part], u_sem.at[side]))
        d_copies.append(pltpu.make_async_copy(downs[side], wd.at[part], d_sem.at[side]))
    for copy in x_copies:
        copy.start()
    for side in range(2):
        g_copies[side].start()
        u_copies[side].start()
    for copy in d_copies:
        copy.start()
    for copy in x_copies:
        copy.wait()
    contract = (((1,), (1,)), ((), ()))
    for side in range(2):
        g_copies[side].wait()
        u_copies[side].wait()
        for start in range(0, hidden, HIDDEN_TILE):
            part = pl.ds(side * hidden + start, min(HIDDEN_TILE, hidden - start))
            gate = lax.dot_general(x[...], wg[part, :], contract, preferred_element_type=F32)
            lifted = lax.dot_general(x[...], wu[part, :], contract, preferred_element_type=F32)
            act[:, part] = (gate / (1.0 + jnp.exp(-gate)) * lifted).astype(BF)
    for copy in d_copies:
        copy.wait()
    cols = D // OUT_TILES
    for j in range(OUT_TILES):
        part = pl.ds(j * cols, cols)
        res[:, part] = jnp.dot(act[...], wd[:, part], preferred_element_type=F32).astype(BF)
    for copy in out_copies:
        copy.start()
    for copy in out_copies:
        copy.wait()


def ffn(pieces, gates, ups, downs):
    rows = tuple(p.shape[0] for p in pieces)
    total, number = sum(rows), len(rows)
    hidden = gates[0].shape[0]
    any_spec = pl.BlockSpec(memory_space=pl.ANY)
    return pl.pallas_call(
        functools.partial(ffn_kernel, rows),
        in_specs=[any_spec] * (number + 6),
        out_specs=[any_spec] * number,
        out_shape=[jax.ShapeDtypeStruct((count, D), BF) for count in rows],
        scratch_shapes=[
            pltpu.VMEM((total, D), BF),
            pltpu.VMEM((2 * hidden, D), BF),
            pltpu.VMEM((2 * hidden, D), BF),
            pltpu.VMEM((2 * hidden, D), BF),
            pltpu.VMEM((total, 2 * hidden), BF),
            pltpu.VMEM((total, D), BF),
            pltpu.SemaphoreType.DMA((number,)),
            pltpu.SemaphoreType.DMA((2,)),
            pltpu.SemaphoreType.DMA((2,)),
            pltpu.SemaphoreType.DMA((2,)),
            pltpu.SemaphoreType.DMA((number,)),
        ],
        compiler_params=pltpu.CompilerParams(vmem_limit_bytes=50 * 1024 * 1024),
        cost_estimate=pl.CostEstimate(
            flops=12 * total * hidden * D, bytes_accessed=12 * hidden * D + 4 * total * D, transcendentals=2 * total * hidden
        ),
    )(*pieces, *gates, *ups, *downs)


def after(values, *others):
    return lax.optimization_barrier((values, others))[0]


def per_device(
    tokens, w_query, w_key, w_value, w_out, w_gate, w_up, w_down, route, old_out, cotangent
):
    experts = 8
    capacity = 2
    length = tokens.shape[0]
    blocks = length // BLOCK
    piece_rows = BLOCK // experts
    old_count = experts - max(1, experts // 4)
    yl, z, core = lax.axis_index("yl"), lax.axis_index("z"), lax.axis_index("core")
    own = yl * 4 + z

    width = D // 2
    own_out = lax.dynamic_slice_in_dim(w_out, core * width, width, 1)
    wa, wb = own_out[:HEAD_DIM], own_out[HEAD_DIM:]
    w1 = gather_start(wa, wb, "z", "yl")
    gates = [w_gate[0], shift(w_gate[0], "core", 1)]
    ups = [w_up[0], shift(w_up[0], "core", 1)]
    downs = [w_down[0], shift(w_down[0], "core", 1)]

    routes = route[:, 0]
    hits = routing_table(routes, experts, capacity)
    table = hits.astype(BF)
    places = jnp.sum(
        hits.astype(jnp.int32) * lax.broadcasted_iota(jnp.int32, hits.shape, 2), axis=2
    )
    mine = lax.dynamic_slice_in_dim(places, own, 1, 0)[0]
    own_tokens = [
        lax.dynamic_slice_in_dim(tokens, mine[slot] * BLOCK, BLOCK, 0) for slot in range(capacity)
    ]

    heads_out = attend_local(tokens, w_query, w_key, w_value)
    payload, heads_out = after((gather_middle(wa, wb, w1), heads_out))
    w2 = gather_send(payload, "z", "yl")
    outgoing = jnp.einsum(
        "jcb,brd->jcrd", table, heads_out.reshape(blocks, BLOCK, -1), preferred_element_type=F32
    ).astype(BF)
    heads_in = lax.all_to_all(
        outgoing.reshape(experts, capacity * BLOCK, -1), ("yl", "z"), split_axis=0, concat_axis=0, tiled=True
    )
    heads_in = rows_of_cores(heads_in)
    terms = lax.dot_general(
        after(cotangent, heads_in), heads_out, (((0,), (0,)), ((), ())), preferred_element_type=F32
    ).astype(BF)
    gradient = sum_terms(terms, core)

    def near(dy, dz):
        at = ((yl + dy) % 2) * 4 + (z + dz) % 4
        return lax.dynamic_slice_in_dim(heads_in, at, 1, 0)[0]

    hd = {(dy, dz): near(dy, dz) for dy in range(2) for dz in (0, -1, 1, 2)}

    def a(dy, dz):
        return hd[dy, dz][:, :HEAD_DIM]

    def b(dy, dz):
        return hd[dy, dz][:, HEAD_DIM:]

    half = HEAD_DIM // 2
    lhs = [
        hd[0, 0],
        a(1, 0),
        b(0, -1),
        b(0, 1),
        jnp.concatenate([a(0, -1), a(1, -1), b(0, 2)[:, :half]], axis=1),
        jnp.concatenate([a(0, 1), a(1, 1), b(0, 2)[:, half:]], axis=1),
        jnp.concatenate([b(1, 0), b(1, -1), b(1, 1)], axis=1),
        a(0, 2),
        a(1, 2),
        b(1, 2),
    ]
    w3 = gather_send(after(gather_last(w2, HEAD_DIM), lhs), "z", "yl")
    attention = project(lhs, [own_out, *w1, *w2, *w3])
    attention, gradient = after((attention, gradient))
    rows = capacity * BLOCK
    here = attention[:rows]
    there = shift(attention[rows:], "core", 1)
    first_half = jnp.where(core == 0, here, there)
    second_half = jnp.where(core == 0, there, here)
    both = jnp.concatenate([first_half, second_half], axis=1)
    ha = plus(own_tokens[0], both[:BLOCK])
    hb = plus(own_tokens[1], both[BLOCK:])

    r1 = gather_start(ha, hb, "x", "yh")
    r2 = gather_send(gather_middle(ha, hb, r1), "x", "yh")
    pa, pb, p_ap, p_bl, p_br = early = ffn([ha, hb, *r1], gates, ups, downs)
    r3 = gather_send(after(gather_last(r2, BLOCK), early), "x", "yh")
    p_left, p_right, p_across = middle = ffn(list(r2), gates, ups, downs)
    p_aa, p_apa, p_bpa = ffn(after(list(r3), middle), gates, ups, downs)

    n, h = BLOCK, BLOCK // 2
    s_aa = shift(p_aa, "x", -1)
    s_apa = shift(p_apa, "x", 1)
    s_bpa = shift(p_bpa, "yh", 1)
    left = rows_of(plus(p_left[:n], s_aa), p_left[n : 2 * n], plus(p_left[2 * n :], s_bpa[:h]))
    right = rows_of(p_right[:n], plus(p_right[n : 2 * n], s_apa), plus(p_right[2 * n :], s_bpa[h:]))
    s_left = shift(left, "x", -1)
    s_right = shift(right, "x", 1)
    s_across = shift(p_across, "yh", 1)
    t_ap = plus(p_ap, s_left[n : 2 * n], s_right[n : 2 * n])
    t_bl = rows_of(plus(p_bl[:h], s_across[n : n + h], s_left[2 * n :]), plus(p_bl[h:], s_across[n + h : 2 * n]))
    t_br = rows_of(plus(p_br[:h], s_across[2 * n : 2 * n + h]), plus(p_br[h:], s_across[2 * n + h :], s_right[2 * n :]))
    e_a = shift(t_ap, "yh", 1)
    e_bl = shift(t_bl, "x", -1)
    e_br = shift(t_br, "x", 1)
    out_a = plus(pa, s_left[:n], s_right[:n], e_a)
    out_b = plus(pb, s_across[:n], e_bl, e_br)

    done = rows_of(plus(ha, out_a), plus(hb, out_b)).reshape(capacity, experts, piece_rows, D)
    returned = lax.all_to_all(
        jnp.moveaxis(done, 1, 0), ("yl", "z"), split_axis=0, concat_axis=0, tiled=True
    )
    joined = jnp.einsum("jcb,jcrd->brd", table, returned, preferred_element_type=F32)
    fresh = (routes >= old_count).astype(F32)
    gap = joined - old_out.astype(F32)
    divergence = 0.5 * jnp.mean(gap * gap, axis=-1) * fresh[:, None]

    return (joined.astype(BF), divergence, gradient)


def sum_terms(terms, core):
    terms = terms.reshape(8, 2, D // 16, -1)
    kept = lax.dynamic_slice_in_dim(terms, core, 1, 1)[:, 0]
    given = lax.dynamic_slice_in_dim(terms, 1 - core, 1, 1)[:, 0]
    pairs = plus(kept, shift(given, "core", 1))
    arrived = lax.all_to_all(pairs, ("x", "yh"), split_axis=0, concat_axis=0, tiled=True)
    return arrived.astype(F32).sum(axis=0)


def rows_of_cores(heads_in):
    return jnp.concatenate([heads_in, shift(heads_in, "core", 1)], axis=1)


def solution(mesh):
    fine = Mesh(mesh.devices.reshape(tuple(SIZES.values())), AXES)
    replica, expert = ("x", "yh", "core"), ("yl", "z")
    return jax.shard_map(
        per_device,
        mesh=fine,
        in_specs=(
            P(replica, None),
            P(None, expert),
            P(None, expert),
            P(None, expert),
            P(expert, None),
            P(expert, replica, None),
            P(expert, replica, None),
            P(expert, replica, None),
            P(replica, None),
            P(replica, expert, None),
            P(replica, None),
        ),
        out_specs=(
            P(replica, expert, None),
            P(replica, expert),
            P(replica, expert),
        ),
        check_vma=False,
    )
```

```python
import functools
import math

import jax
import jax.numpy as jnp
from jax import lax
from jax.experimental import pallas as pl
from jax.experimental.pallas import tpu as pltpu
from jax.sharding import Mesh
from jax.sharding import PartitionSpec as P

D = 4096
HEAD_DIM = 128
BLOCK = 64
SIZES = {"x": 4, "yh": 2, "core": 2, "yl": 2, "z": 4}
AXES = ("x", "yh", "core", "yl", "z")
BF = jnp.bfloat16
F32 = jnp.float32


def shift(value, axis, by):
    n = SIZES[axis]
    return lax.ppermute(value, axis, [(i, (i + by) % n) for i in range(n)])


def rows_of(*parts):
    return jnp.concatenate(parts, axis=0)


def plus(first, *others):
    total = first.astype(F32)
    for other in others:
        total = total + other.astype(F32)
    return total.astype(BF)


def attend_kernel(tokens, w_query, w_key, w_value, out):
    length = tokens.shape[0]
    queries = jnp.dot(tokens[...], w_query[...], preferred_element_type=F32).astype(BF)
    keys = jnp.dot(tokens[...], w_key[...], preferred_element_type=F32).astype(BF)
    values = jnp.dot(tokens[...], w_value[...], preferred_element_type=F32).astype(BF)
    query_pos = lax.broadcasted_iota(jnp.int32, (length, length), 0)
    key_pos = lax.broadcasted_iota(jnp.int32, (length, length), 1)
    seen = query_pos >= key_pos
    for head in range(w_query.shape[1] // HEAD_DIM):
        part = slice(head * HEAD_DIM, (head + 1) * HEAD_DIM)
        scores = lax.dot_general(
            queries[:, part], keys, (((1,), (1,)), ((), ())), preferred_element_type=F32
        ) * (1.0 / math.sqrt(HEAD_DIM))
        scores = jnp.where(seen, scores, -jnp.inf)
        top = jnp.max(scores, axis=-1, keepdims=True)
        weights = jnp.exp(scores - top)
        probs = (weights / jnp.sum(weights, axis=-1, keepdims=True)).astype(BF)
        out[:, part] = jnp.dot(probs, values, preferred_element_type=F32).astype(BF)


def attend_local(tokens, w_query, w_key, w_value):
    length, columns = tokens.shape[0], w_query.shape[1]
    return pl.pallas_call(
        attend_kernel,
        in_specs=[pl.BlockSpec(memory_space=pltpu.VMEM)] * 4,
        out_specs=pl.BlockSpec(memory_space=pltpu.VMEM),
        out_shape=jax.ShapeDtypeStruct((length, columns), BF),
        compiler_params=pltpu.CompilerParams(vmem_limit_bytes=48 * 1024 * 1024),
        cost_estimate=pl.CostEstimate(
            flops=4 * length * D * columns, bytes_accessed=2 * D * (length + 2 * columns), transcendentals=length * length * 2
        ),
    )(tokens, w_query, w_key, w_value)


def routing_table(routes, experts, capacity):
    number = routes.shape[0]
    same = routes[:, None] == routes[None, :]
    earlier = lax.broadcasted_iota(jnp.int32, (number, number), 1) < lax.broadcasted_iota(
        jnp.int32, (number, number), 0
    )
    slot = jnp.sum((same & earlier).astype(jnp.int32), axis=1)
    expert_hit = routes[None, :] == lax.broadcasted_iota(jnp.int32, (experts, number), 0)
    slot_hit = slot[None, :] == lax.broadcasted_iota(jnp.int32, (capacity, number), 0)
    return expert_hit[:, None, :] & slot_hit[None, :, :]


def gather_start(first, second, ring, pair):
    return shift(first, pair, 1), shift(second, ring, 1), shift(second, ring, -1)


def gather_middle(first, second, arrived):
    first_p, second_l, second_r = arrived
    half = second.shape[0] // 2
    return (
        rows_of(first, first_p, second_l[:half]),
        rows_of(first, first_p, second_r[half:]),
        rows_of(second, second_l, second_r),
    )


def gather_send(payload, ring, pair):
    return shift(payload[0], ring, 1), shift(payload[1], ring, -1), shift(payload[2], pair, 1)


def gather_last(arrived, n):
    left, right, _ = arrived
    return left[:n], right[n : 2 * n], rows_of(left[2 * n :], right[2 * n :])


def project_kernel(number, *refs):
    lhs, weights, out = refs[:number], refs[number : 2 * number], refs[2 * number]
    total = jnp.zeros(out.shape, F32)
    for left, right in zip(lhs, weights):
        total = total + jnp.dot(left[...], right[...], preferred_element_type=F32)
    out[...] = total.astype(BF)


def project(lhs, weights):
    rows, width = lhs[0].shape[0], weights[0].shape[1]
    tile = 512
    number = len(lhs)
    depth = sum(w.shape[0] for w in weights)
    return pl.pallas_call(
        functools.partial(project_kernel, number),
        grid=(width // tile,),
        in_specs=[pl.BlockSpec(v.shape, lambda j: (0, 0)) for v in lhs]
        + [pl.BlockSpec((w.shape[0], tile), lambda j: (0, j)) for w in weights],
        out_specs=pl.BlockSpec((rows, tile), lambda j: (0, j)),
        out_shape=jax.ShapeDtypeStruct((rows, width), BF),
        compiler_params=pltpu.CompilerParams(vmem_limit_bytes=60 * 1024 * 1024),
        cost_estimate=pl.CostEstimate(
            flops=2 * rows * width * depth, bytes_accessed=2 * depth * (rows + width), transcendentals=0
        ),
    )(*lhs, *weights)


OUT_TILES = 4
HIDDEN_TILE = 256


def ffn_kernel(rows, out_rows, *refs):
    number = len(rows)
    pieces = refs[:number]
    gates, ups, downs = refs[number : number + 2], refs[number + 2 : number + 4], refs[number + 4 : number + 6]
    outs = refs[number + 6 : number + 6 + len(out_rows)]
    x, wg, wu, wd, act, res, x_sem, g_sem, u_sem, d_sem, o_sem = refs[number + 6 + len(out_rows) :]
    hidden = gates[0].shape[0]

    x_copies, out_copies = [], []
    start = 0
    for i, count in enumerate(rows):
        part = pl.ds(start, count)
        x_copies.append(pltpu.make_async_copy(pieces[i], x.at[part], x_sem.at[i]))
        start += count
    start = 0
    for i, count in enumerate(out_rows):
        part = pl.ds(start, count)
        out_copies.append(pltpu.make_async_copy(res.at[part], outs[i], o_sem.at[i]))
        start += count
    g_copies, u_copies, d_copies = [], [], []
    for side in range(2):
        part = pl.ds(side * hidden, hidden)
        g_copies.append(pltpu.make_async_copy(gates[side], wg.at[part], g_sem.at[side]))
        u_copies.append(pltpu.make_async_copy(ups[side], wu.at[part], u_sem.at[side]))
        d_copies.append(pltpu.make_async_copy(downs[side], wd.at[part], d_sem.at[side]))
    for copy in x_copies:
        copy.start()
    for side in range(2):
        g_copies[side].start()
        u_copies[side].start()
    for copy in d_copies:
        copy.start()
    for copy in x_copies:
        copy.wait()
    contract = (((1,), (1,)), ((), ()))
    for side in range(2):
        g_copies[side].wait()
        u_copies[side].wait()
        for start in range(0, hidden, HIDDEN_TILE):
            part = pl.ds(side * hidden + start, min(HIDDEN_TILE, hidden - start))
            gate = lax.dot_general(x[...], wg[part, :], contract, preferred_element_type=F32)
            lifted = lax.dot_general(x[...], wu[part, :], contract, preferred_element_type=F32)
            act[:, part] = (gate / (1.0 + jnp.exp(-gate)) * lifted).astype(BF)
    for copy in d_copies:
        copy.wait()
    cols = D // OUT_TILES
    for j in range(OUT_TILES):
        part = pl.ds(j * cols, cols)
        res[:, part] = jnp.dot(act[...], wd[:, part], preferred_element_type=F32).astype(BF)
    for copy in out_copies:
        copy.start()
    for copy in out_copies:
        copy.wait()


def ffn(pieces, gates, ups, downs, out_rows=None):
    rows = tuple(p.shape[0] for p in pieces)
    out_rows = out_rows or rows
    total, number = sum(rows), len(rows)
    hidden = gates[0].shape[0]
    hbm_spec = pl.BlockSpec(memory_space=pltpu.HBM)
    return pl.pallas_call(
        functools.partial(ffn_kernel, rows, out_rows),
        in_specs=[hbm_spec] * (number + 6),
        out_specs=[hbm_spec] * len(out_rows),
        out_shape=[jax.ShapeDtypeStruct((count, D), BF) for count in out_rows],
        scratch_shapes=[
            pltpu.VMEM((total, D), BF),
            pltpu.VMEM((2 * hidden, D), BF),
            pltpu.VMEM((2 * hidden, D), BF),
            pltpu.VMEM((2 * hidden, D), BF),
            pltpu.VMEM((total, 2 * hidden), BF),
            pltpu.VMEM((total, D), BF),
            pltpu.SemaphoreType.DMA((number,)),
            pltpu.SemaphoreType.DMA((2,)),
            pltpu.SemaphoreType.DMA((2,)),
            pltpu.SemaphoreType.DMA((2,)),
            pltpu.SemaphoreType.DMA((len(out_rows),)),
        ],
        compiler_params=pltpu.CompilerParams(vmem_limit_bytes=60 * 1024 * 1024),
        cost_estimate=pl.CostEstimate(
            flops=12 * total * hidden * D, bytes_accessed=12 * hidden * D + 4 * total * D, transcendentals=2 * total * hidden
        ),
    )(*pieces, *gates, *ups, *downs)


def after(values, *others):
    return lax.optimization_barrier((values, others))[0]


def per_device(
    tokens, w_query, w_key, w_value, w_out, w_gate, w_up, w_down, route, old_out, cotangent
):
    experts = 8
    capacity = 2
    length = tokens.shape[0]
    blocks = length // BLOCK
    piece_rows = BLOCK // experts
    old_count = experts - max(1, experts // 4)
    yl, z, core = lax.axis_index("yl"), lax.axis_index("z"), lax.axis_index("core")
    own = yl * 4 + z

    width = D // 2
    own_out = lax.dynamic_slice_in_dim(w_out, core * width, width, 1)
    wa, wb = own_out[:HEAD_DIM], own_out[HEAD_DIM:]
    w1 = gather_start(wa, wb, "z", "yl")
    gates = [w_gate[0], shift(w_gate[0], "core", 1)]

    routes = route[:, 0]
    hits = routing_table(routes, experts, capacity)
    table = hits.astype(BF)
    places = jnp.sum(
        hits.astype(jnp.int32) * lax.broadcasted_iota(jnp.int32, hits.shape, 2), axis=2
    )
    mine = lax.dynamic_slice_in_dim(places, own, 1, 0)[0]
    own_tokens = [
        lax.dynamic_slice_in_dim(tokens, mine[slot] * BLOCK, BLOCK, 0) for slot in range(capacity)
    ]

    heads_out = attend_local(tokens, w_query, w_key, w_value)
    outgoing = jnp.einsum(
        "jcb,brd->jcrd", table, heads_out.reshape(blocks, BLOCK, -1), preferred_element_type=F32
    ).astype(BF)
    heads_in = lax.all_to_all(
        outgoing.reshape(experts, capacity * BLOCK, -1), ("yl", "z"), split_axis=0, concat_axis=0, tiled=True
    )
    payload, heads_in = after((gather_middle(wa, wb, w1), heads_in), gates[1])
    w2 = gather_send(payload, "z", "yl")
    heads_in = rows_of_cores(heads_in)

    def near(dy, dz):
        at = ((yl + dy) % 2) * 4 + (z + dz) % 4
        return lax.dynamic_slice_in_dim(heads_in, at, 1, 0)[0]

    hd = {(dy, dz): near(dy, dz) for dy in range(2) for dz in (0, -1, 1, 2)}

    def a(dy, dz):
        return hd[dy, dz][:, :HEAD_DIM]

    def b(dy, dz):
        return hd[dy, dz][:, HEAD_DIM:]

    half = HEAD_DIM // 2
    lhs = [
        hd[0, 0],
        a(1, 0),
        b(0, -1),
        b(0, 1),
        jnp.concatenate([a(0, -1), a(1, -1), b(0, 2)[:, :half]], axis=1),
        jnp.concatenate([a(0, 1), a(1, 1), b(0, 2)[:, half:]], axis=1),
        jnp.concatenate([b(1, 0), b(1, -1), b(1, 1)], axis=1),
        a(0, 2),
        a(1, 2),
        b(1, 2),
    ]
    w2, lhs = after((w2, lhs))
    last = gather_last(w2, HEAD_DIM)
    w3 = gather_send(last, "z", "yl")
    ups = [w_up[0], shift(after(w_up[0], last), "core", 1)]
    terms = lax.dot_general(
        after(cotangent, last), heads_out, (((0,), (0,)), ((), ())), preferred_element_type=F32
    ).astype(BF)
    w3, lhs, terms = after((w3, lhs, terms.reshape(8, 2, D // 16, -1)), ups[1])
    attention = project(lhs, [own_out, *w1, *w2, *w3])
    rows = capacity * BLOCK
    here = attention[:rows]
    there = shift(attention[rows:], "core", 1)
    first_half = jnp.where(core == 0, here, there)
    second_half = jnp.where(core == 0, there, here)
    both = jnp.concatenate([first_half, second_half], axis=1)
    ha = plus(own_tokens[0], both[:BLOCK])
    hb = plus(own_tokens[1], both[BLOCK:])

    downs = [w_down[0], shift(after(w_down[0], (ha, hb)), "core", 1)]
    r1 = gather_start(ha, hb, "x", "yh")
    first = after(gather_middle(ha, hb, r1), downs[1])
    r2 = gather_send(first, "x", "yh")
    pa, pb, p_ap, p_bl, p_br = early = ffn([ha, hb, *r1], gates, ups, downs)
    kept, given = halves(terms, 1, core)
    pairs = plus(kept, shift(given, "core", 1)).reshape(4, 2, D // 16, -1)
    last, left_right, pairs = after((gather_last(r2, BLOCK), list(r2[:2]), pairs), early)
    r3 = gather_send(last, "x", "yh")
    kept, given = halves(pairs, 1, lax.axis_index("yh"))
    quads = plus(kept, shift(given, "yh", 1))
    x = lax.axis_index("x")
    term = [lax.dynamic_slice_in_dim(quads, (x + k) % 4, 1, 0)[0] for k in range(4)]
    middle = ffn(left_right, gates, ups, downs)
    late, (p_left, p_right), term = after(([r2[2], *r3], middle, term))
    p_middle, p_sides, p_aa, p_apa, p_bpa = ffn(late, gates, ups, downs, (BLOCK, 2 * BLOCK, BLOCK, BLOCK, BLOCK))

    n, h = BLOCK, BLOCK // 2
    s_aa = shift(p_aa, "x", -1)
    s_apa = shift(p_apa, "x", 1)
    s_bpa = shift(p_bpa, "yh", 1)
    left = rows_of(plus(p_left[:n], s_aa), p_left[n : 2 * n], plus(p_left[2 * n :], s_bpa[:h]))
    right = rows_of(p_right[:n], plus(p_right[n : 2 * n], s_apa), plus(p_right[2 * n :], s_bpa[h:]))
    s_left = shift(left, "x", -1)
    s_right = shift(right, "x", 1)
    s_sides = shift(p_sides, "yh", 1)
    s_middle = shift(after(p_middle, s_sides), "yh", 1)
    t_ap = plus(p_ap, s_left[n : 2 * n], s_right[n : 2 * n])
    t_bl = rows_of(plus(p_bl[:h], s_sides[:h], s_left[2 * n :]), plus(p_bl[h:], s_sides[h:n]))
    t_br = rows_of(plus(p_br[:h], s_sides[n : n + h]), plus(p_br[h:], s_sides[n + h :], s_right[2 * n :]))
    e_a = shift(t_ap, "yh", 1)
    e_bl = shift(t_bl, "x", -1)
    e_br = shift(t_br, "x", 1)
    out_a = plus(pa, s_left[:n], s_right[:n], e_a)
    out_b = plus(pb, s_middle, e_bl, e_br)

    done = rows_of(plus(ha, out_a), plus(hb, out_b)).reshape(capacity, experts, piece_rows, D)
    done, term = after((done, term))
    met = [shift(term[k], "x", k) for k in range(1, 4)]
    gradient = term[0].astype(F32) + met[0].astype(F32) + met[1].astype(F32) + met[2].astype(F32)
    returned = lax.all_to_all(
        jnp.moveaxis(done, 1, 0), ("yl", "z"), split_axis=0, concat_axis=0, tiled=True
    )
    joined = jnp.einsum("jcb,jcrd->brd", table, returned, preferred_element_type=F32)
    fresh = (routes >= old_count).astype(F32)
    gap = joined - old_out.astype(F32)
    divergence = 0.5 * jnp.mean(gap * gap, axis=-1) * fresh[:, None]

    return (joined.astype(BF), divergence, gradient)


def halves(value, axis, index):
    return (
        jnp.squeeze(lax.dynamic_slice_in_dim(value, index, 1, axis), axis),
        jnp.squeeze(lax.dynamic_slice_in_dim(value, 1 - index, 1, axis), axis),
    )


def rows_of_cores(heads_in):
    return jnp.concatenate([heads_in, shift(heads_in, "core", 1)], axis=1)


def solution(mesh):
    fine = Mesh(mesh.devices.reshape(tuple(SIZES.values())), AXES)
    replica, expert = ("x", "yh", "core"), ("yl", "z")
    return jax.shard_map(
        per_device,
        mesh=fine,
        in_specs=(
            P(replica, None),
            P(None, expert),
            P(None, expert),
            P(None, expert),
            P(expert, None),
            P(expert, replica, None),
            P(expert, replica, None),
            P(expert, replica, None),
            P(replica, None),
            P(replica, expert, None),
            P(replica, None),
        ),
        out_specs=(
            P(replica, expert, None),
            P(replica, expert),
            P(replica, expert),
        ),
        check_vma=False,
    )
```

```python
import functools
import math

import jax
import jax.numpy as jnp
from jax import lax
from jax.experimental import pallas as pl
from jax.experimental.pallas import tpu as pltpu
from jax.sharding import Mesh
from jax.sharding import PartitionSpec as P

D = 4096
HEAD_DIM = 128
BLOCK = 64
SIZES = {"x": 4, "yh": 2, "core": 2, "yl": 2, "z": 4}
AXES = ("x", "yh", "core", "yl", "z")
BF = jnp.bfloat16
F32 = jnp.float32


def shift(value, axis, by):
    n = SIZES[axis]
    return lax.ppermute(value, axis, [(i, (i + by) % n) for i in range(n)])


def rows_of(*parts):
    return jnp.concatenate(parts, axis=0)


def plus(first, *others):
    total = first.astype(F32)
    for other in others:
        total = total + other.astype(F32)
    return total.astype(BF)


def attend_kernel(tokens, w_query, w_key, w_value, out):
    length = tokens.shape[0]
    queries = jnp.dot(tokens[...], w_query[...], preferred_element_type=F32).astype(BF)
    keys = jnp.dot(tokens[...], w_key[...], preferred_element_type=F32).astype(BF)
    values = jnp.dot(tokens[...], w_value[...], preferred_element_type=F32).astype(BF)
    query_pos = lax.broadcasted_iota(jnp.int32, (length, length), 0)
    key_pos = lax.broadcasted_iota(jnp.int32, (length, length), 1)
    seen = query_pos >= key_pos
    for head in range(w_query.shape[1] // HEAD_DIM):
        part = slice(head * HEAD_DIM, (head + 1) * HEAD_DIM)
        scores = lax.dot_general(
            queries[:, part], keys, (((1,), (1,)), ((), ())), preferred_element_type=F32
        ) * (1.0 / math.sqrt(HEAD_DIM))
        scores = jnp.where(seen, scores, -jnp.inf)
        top = jnp.max(scores, axis=-1, keepdims=True)
        weights = jnp.exp(scores - top)
        probs = (weights / jnp.sum(weights, axis=-1, keepdims=True)).astype(BF)
        out[:, part] = jnp.dot(probs, values, preferred_element_type=F32).astype(BF)


def attend_local(tokens, w_query, w_key, w_value):
    length, columns = tokens.shape[0], w_query.shape[1]
    return pl.pallas_call(
        attend_kernel,
        in_specs=[pl.BlockSpec(memory_space=pltpu.VMEM)] * 4,
        out_specs=pl.BlockSpec(memory_space=pltpu.VMEM),
        out_shape=jax.ShapeDtypeStruct((length, columns), BF),
        compiler_params=pltpu.CompilerParams(vmem_limit_bytes=48 * 1024 * 1024),
        cost_estimate=pl.CostEstimate(
            flops=4 * length * D * columns, bytes_accessed=2 * D * (length + 2 * columns), transcendentals=length * length * 2
        ),
    )(tokens, w_query, w_key, w_value)


def routing_table(routes, experts, capacity):
    number = routes.shape[0]
    same = routes[:, None] == routes[None, :]
    earlier = lax.broadcasted_iota(jnp.int32, (number, number), 1) < lax.broadcasted_iota(
        jnp.int32, (number, number), 0
    )
    slot = jnp.sum((same & earlier).astype(jnp.int32), axis=1)
    expert_hit = routes[None, :] == lax.broadcasted_iota(jnp.int32, (experts, number), 0)
    slot_hit = slot[None, :] == lax.broadcasted_iota(jnp.int32, (capacity, number), 0)
    return expert_hit[:, None, :] & slot_hit[None, :, :]


def gather_start(first, second, ring, pair):
    return shift(first, pair, 1), shift(second, ring, 1), shift(second, ring, -1)


def gather_middle(first, second, arrived):
    first_p, second_l, second_r = arrived
    half = second.shape[0] // 2
    return (
        rows_of(first, first_p, second_l[:half]),
        rows_of(first, first_p, second_r[half:]),
        rows_of(second, second_l, second_r),
    )


def gather_send(payload, ring, pair):
    return shift(payload[0], ring, 1), shift(payload[1], ring, -1), shift(payload[2], pair, 1)


def gather_last(arrived, n):
    left, right, _ = arrived
    return left[:n], right[n : 2 * n], rows_of(left[2 * n :], right[2 * n :])


def project_kernel(number, *refs):
    lhs, weights, out = refs[:number], refs[number : 2 * number], refs[2 * number]
    total = jnp.zeros(out.shape, F32)
    for left, right in zip(lhs, weights):
        total = total + jnp.dot(left[...], right[...], preferred_element_type=F32)
    out[...] = total.astype(BF)


def project(lhs, weights):
    rows, width = lhs[0].shape[0], weights[0].shape[1]
    tile = 512
    number = len(lhs)
    depth = sum(w.shape[0] for w in weights)
    return pl.pallas_call(
        functools.partial(project_kernel, number),
        grid=(width // tile,),
        in_specs=[pl.BlockSpec(v.shape, lambda j: (0, 0)) for v in lhs]
        + [pl.BlockSpec((w.shape[0], tile), lambda j: (0, j)) for w in weights],
        out_specs=pl.BlockSpec((rows, tile), lambda j: (0, j)),
        out_shape=jax.ShapeDtypeStruct((rows, width), BF),
        compiler_params=pltpu.CompilerParams(vmem_limit_bytes=60 * 1024 * 1024),
        cost_estimate=pl.CostEstimate(
            flops=2 * rows * width * depth, bytes_accessed=2 * depth * (rows + width), transcendentals=0
        ),
    )(*lhs, *weights)


OUT_TILES = 4
HIDDEN_TILE = 256


def ffn_kernel(rows, out_rows, *refs):
    number = len(rows)
    pieces = refs[:number]
    gates, ups, downs = refs[number : number + 2], refs[number + 2 : number + 4], refs[number + 4 : number + 6]
    outs = refs[number + 6 : number + 6 + len(out_rows)]
    x, wg, wu, wd, act, res, x_sem, g_sem, u_sem, d_sem, o_sem = refs[number + 6 + len(out_rows) :]
    hidden = gates[0].shape[0]

    x_copies, out_copies = [], []
    start = 0
    for i, count in enumerate(rows):
        part = pl.ds(start, count)
        x_copies.append(pltpu.make_async_copy(pieces[i], x.at[part], x_sem.at[i]))
        start += count
    start = 0
    for i, count in enumerate(out_rows):
        part = pl.ds(start, count)
        out_copies.append(pltpu.make_async_copy(res.at[part], outs[i], o_sem.at[i]))
        start += count
    g_copies, u_copies, d_copies = [], [], []
    for side in range(2):
        part = pl.ds(side * hidden, hidden)
        g_copies.append(pltpu.make_async_copy(gates[side], wg.at[part], g_sem.at[side]))
        u_copies.append(pltpu.make_async_copy(ups[side], wu.at[part], u_sem.at[side]))
        d_copies.append(pltpu.make_async_copy(downs[side], wd.at[part], d_sem.at[side]))
    for copy in x_copies:
        copy.start()
    for side in range(2):
        g_copies[side].start()
        u_copies[side].start()
    for copy in d_copies:
        copy.start()
    for copy in x_copies:
        copy.wait()
    contract = (((1,), (1,)), ((), ()))
    for side in range(2):
        g_copies[side].wait()
        u_copies[side].wait()
        for start in range(0, hidden, HIDDEN_TILE):
            part = pl.ds(side * hidden + start, min(HIDDEN_TILE, hidden - start))
            gate = lax.dot_general(x[...], wg[part, :], contract, preferred_element_type=F32)
            lifted = lax.dot_general(x[...], wu[part, :], contract, preferred_element_type=F32)
            act[:, part] = (gate / (1.0 + jnp.exp(-gate)) * lifted).astype(BF)
    for copy in d_copies:
        copy.wait()
    cols = D // OUT_TILES
    for j in range(OUT_TILES):
        part = pl.ds(j * cols, cols)
        res[:, part] = jnp.dot(act[...], wd[:, part], preferred_element_type=F32).astype(BF)
    for copy in out_copies:
        copy.start()
    for copy in out_copies:
        copy.wait()


def ffn(pieces, gates, ups, downs, out_rows=None):
    rows = tuple(p.shape[0] for p in pieces)
    out_rows = out_rows or rows
    total, number = sum(rows), len(rows)
    hidden = gates[0].shape[0]
    hbm_spec = pl.BlockSpec(memory_space=pltpu.HBM)
    return pl.pallas_call(
        functools.partial(ffn_kernel, rows, out_rows),
        in_specs=[hbm_spec] * (number + 6),
        out_specs=[hbm_spec] * len(out_rows),
        out_shape=[jax.ShapeDtypeStruct((count, D), BF) for count in out_rows],
        scratch_shapes=[
            pltpu.VMEM((total, D), BF),
            pltpu.VMEM((2 * hidden, D), BF),
            pltpu.VMEM((2 * hidden, D), BF),
            pltpu.VMEM((2 * hidden, D), BF),
            pltpu.VMEM((total, 2 * hidden), BF),
            pltpu.VMEM((total, D), BF),
            pltpu.SemaphoreType.DMA((number,)),
            pltpu.SemaphoreType.DMA((2,)),
            pltpu.SemaphoreType.DMA((2,)),
            pltpu.SemaphoreType.DMA((2,)),
            pltpu.SemaphoreType.DMA((len(out_rows),)),
        ],
        compiler_params=pltpu.CompilerParams(vmem_limit_bytes=60 * 1024 * 1024),
        cost_estimate=pl.CostEstimate(
            flops=12 * total * hidden * D, bytes_accessed=12 * hidden * D + 4 * total * D, transcendentals=2 * total * hidden
        ),
    )(*pieces, *gates, *ups, *downs)


def after(values, *others):
    return lax.optimization_barrier((values, others))[0]


def per_device(
    tokens, w_query, w_key, w_value, w_out, w_gate, w_up, w_down, route, old_out, cotangent
):
    experts = 8
    capacity = 2
    length = tokens.shape[0]
    blocks = length // BLOCK
    piece_rows = BLOCK // experts
    old_count = experts - max(1, experts // 4)
    yl, z, core = lax.axis_index("yl"), lax.axis_index("z"), lax.axis_index("core")
    own = yl * 4 + z

    width = D // 2
    own_out = lax.dynamic_slice_in_dim(w_out, core * width, width, 1)
    wa, wb = own_out[:HEAD_DIM], own_out[HEAD_DIM:]
    w1 = gather_start(wa, wb, "z", "yl")
    gates = [w_gate[0], shift(w_gate[0], "core", 1)]

    routes = route[:, 0]
    hits = routing_table(routes, experts, capacity)
    table = hits.astype(BF)
    places = jnp.sum(
        hits.astype(jnp.int32) * lax.broadcasted_iota(jnp.int32, hits.shape, 2), axis=2
    )
    mine = lax.dynamic_slice_in_dim(places, own, 1, 0)[0]
    own_tokens = [
        lax.dynamic_slice_in_dim(tokens, mine[slot] * BLOCK, BLOCK, 0) for slot in range(capacity)
    ]

    heads_out = attend_local(tokens, w_query, w_key, w_value)
    outgoing = jnp.einsum(
        "jcb,brd->jcrd", table, heads_out.reshape(blocks, BLOCK, -1), preferred_element_type=F32
    ).astype(BF)
    heads_in = lax.all_to_all(
        outgoing.reshape(experts, capacity * BLOCK, -1), ("yl", "z"), split_axis=0, concat_axis=0, tiled=True
    )
    payload, heads_in = after((gather_middle(wa, wb, w1), heads_in), gates[1])
    w2 = gather_send(payload, "z", "yl")
    heads_in = rows_of_cores(heads_in)

    def near(dy, dz):
        at = ((yl + dy) % 2) * 4 + (z + dz) % 4
        return lax.dynamic_slice_in_dim(heads_in, at, 1, 0)[0]

    hd = {(dy, dz): near(dy, dz) for dy in range(2) for dz in (0, -1, 1, 2)}

    def a(dy, dz):
        return hd[dy, dz][:, :HEAD_DIM]

    def b(dy, dz):
        return hd[dy, dz][:, HEAD_DIM:]

    half = HEAD_DIM // 2
    lhs = [
        hd[0, 0],
        a(1, 0),
        b(0, -1),
        b(0, 1),
        jnp.concatenate([a(0, -1), a(1, -1), b(0, 2)[:, :half]], axis=1),
        jnp.concatenate([a(0, 1), a(1, 1), b(0, 2)[:, half:]], axis=1),
        jnp.concatenate([b(1, 0), b(1, -1), b(1, 1)], axis=1),
        a(0, 2),
        a(1, 2),
        b(1, 2),
    ]
    w2, lhs = after((w2, lhs))
    last = gather_last(w2, HEAD_DIM)
    w3 = gather_send(last, "z", "yl")
    ups = [w_up[0], shift(after(w_up[0], last), "core", 1)]
    terms = lax.dot_general(
        after(cotangent, last), heads_out, (((0,), (0,)), ((), ())), preferred_element_type=F32
    ).astype(BF)
    w3, lhs, terms = after((w3, lhs, terms.reshape(8, 2, D // 16, -1)), ups[1])
    attention = project(lhs, [own_out, *w1, *w2, *w3])
    rows = capacity * BLOCK
    here = attention[:rows]
    there = shift(attention[rows:], "core", 1)
    first_half = jnp.where(core == 0, here, there)
    second_half = jnp.where(core == 0, there, here)
    both = jnp.concatenate([first_half, second_half], axis=1)
    ha = plus(own_tokens[0], both[:BLOCK])
    hb = plus(own_tokens[1], both[BLOCK:])

    downs = [w_down[0], shift(after(w_down[0], w3), "core", 1)]
    r1 = gather_start(ha, hb, "x", "yh")
    kept, given = halves(terms, 1, core)
    pairs = plus(kept, shift(given, "core", 1)).reshape(4, 2, D // 16, -1)
    first, pairs = after((gather_middle(ha, hb, r1), pairs), downs[1])
    r2 = gather_send(first, "x", "yh")
    pa, pb, p_ap, p_bl, p_br = early = ffn([ha, hb, *r1], gates, ups, downs)
    last, left_right, pairs = after((gather_last(r2, BLOCK), list(r2[:2]), pairs), early)
    r3 = gather_send(last, "x", "yh")
    kept, given = halves(pairs, 1, lax.axis_index("yh"))
    quads = plus(kept, shift(given, "yh", 1))
    x = lax.axis_index("x")
    term = [lax.dynamic_slice_in_dim(quads, (x + k) % 4, 1, 0)[0] for k in range(4)]
    middle = ffn(left_right, gates, ups, downs)
    late, (p_left, p_right), term = after(([r2[2], *r3], middle, term))
    p_middle, p_sides, p_aa, p_apa, p_bpa = ffn(late, gates, ups, downs, (BLOCK, 2 * BLOCK, BLOCK, BLOCK, BLOCK))

    n, h = BLOCK, BLOCK // 2
    s_aa = shift(p_aa, "x", -1)
    s_apa = shift(p_apa, "x", 1)
    s_bpa = shift(p_bpa, "yh", 1)
    left = rows_of(plus(p_left[:n], s_aa), p_left[n : 2 * n], plus(p_left[2 * n :], s_bpa[:h]))
    right = rows_of(p_right[:n], plus(p_right[n : 2 * n], s_apa), plus(p_right[2 * n :], s_bpa[h:]))
    s_left = shift(left, "x", -1)
    s_right = shift(right, "x", 1)
    s_sides = shift(p_sides, "yh", 1)
    s_middle = shift(after(p_middle, s_sides), "yh", 1)
    t_ap = plus(p_ap, s_left[n : 2 * n], s_right[n : 2 * n])
    t_bl = rows_of(plus(p_bl[:h], s_sides[:h], s_left[2 * n :]), plus(p_bl[h:], s_sides[h:n]))
    t_br = rows_of(plus(p_br[:h], s_sides[n : n + h]), plus(p_br[h:], s_sides[n + h :], s_right[2 * n :]))
    e_a = shift(t_ap, "yh", 1)
    e_bl = shift(t_bl, "x", -1)
    e_br = shift(t_br, "x", 1)
    out_a = plus(pa, s_left[:n], s_right[:n], e_a)
    out_b = plus(pb, s_middle, e_bl, e_br)

    done = rows_of(plus(ha, out_a), plus(hb, out_b)).reshape(capacity, experts, piece_rows, D)
    done, term = after((done, term))
    met = [shift(term[k], "x", k) for k in range(1, 4)]
    gradient = term[0].astype(F32) + met[0].astype(F32) + met[1].astype(F32) + met[2].astype(F32)
    returned = lax.all_to_all(
        jnp.moveaxis(done, 1, 0), ("yl", "z"), split_axis=0, concat_axis=0, tiled=True
    )
    joined = jnp.einsum("jcb,jcrd->brd", table, returned, preferred_element_type=F32)
    fresh = (routes >= old_count).astype(F32)
    gap = joined - old_out.astype(F32)
    divergence = 0.5 * jnp.mean(gap * gap, axis=-1) * fresh[:, None]

    return (joined.astype(BF), divergence, gradient)


def halves(value, axis, index):
    return (
        jnp.squeeze(lax.dynamic_slice_in_dim(value, index, 1, axis), axis),
        jnp.squeeze(lax.dynamic_slice_in_dim(value, 1 - index, 1, axis), axis),
    )


def rows_of_cores(heads_in):
    return jnp.concatenate([heads_in, shift(heads_in, "core", 1)], axis=1)


def solution(mesh):
    fine = Mesh(mesh.devices.reshape(tuple(SIZES.values())), AXES)
    replica, expert = ("x", "yh", "core"), ("yl", "z")
    return jax.shard_map(
        per_device,
        mesh=fine,
        in_specs=(
            P(replica, None),
            P(None, expert),
            P(None, expert),
            P(None, expert),
            P(expert, None),
            P(expert, replica, None),
            P(expert, replica, None),
            P(expert, replica, None),
            P(replica, None),
            P(replica, expert, None),
            P(replica, None),
        ),
        out_specs=(
            P(replica, expert, None),
            P(replica, expert),
            P(replica, expert),
        ),
        check_vma=False,
    )
```

```python
import functools
import math

import jax
import jax.numpy as jnp
from jax import lax
from jax.experimental import pallas as pl
from jax.experimental.pallas import tpu as pltpu
from jax.sharding import Mesh
from jax.sharding import PartitionSpec as P

D = 4096
HEAD_DIM = 128
BLOCK = 64
SIZES = {"x": 4, "yh": 2, "core": 2, "yl": 2, "z": 4}
AXES = ("x", "yh", "core", "yl", "z")
BF = jnp.bfloat16
F32 = jnp.float32


def shift(value, axis, by):
    n = SIZES[axis]
    return lax.ppermute(value, axis, [(i, (i + by) % n) for i in range(n)])


def rows_of(*parts):
    return jnp.concatenate(parts, axis=0)


def plus(first, *others):
    total = first.astype(F32)
    for other in others:
        total = total + other.astype(F32)
    return total.astype(BF)


def attend_kernel(tokens, w_query, w_key, w_value, out):
    length = tokens.shape[0]
    queries = jnp.dot(tokens[...], w_query[...], preferred_element_type=F32).astype(BF)
    keys = jnp.dot(tokens[...], w_key[...], preferred_element_type=F32).astype(BF)
    values = jnp.dot(tokens[...], w_value[...], preferred_element_type=F32).astype(BF)
    query_pos = lax.broadcasted_iota(jnp.int32, (length, length), 0)
    key_pos = lax.broadcasted_iota(jnp.int32, (length, length), 1)
    seen = query_pos >= key_pos
    for head in range(w_query.shape[1] // HEAD_DIM):
        part = slice(head * HEAD_DIM, (head + 1) * HEAD_DIM)
        scores = lax.dot_general(
            queries[:, part], keys, (((1,), (1,)), ((), ())), preferred_element_type=F32
        ) * (1.0 / math.sqrt(HEAD_DIM))
        scores = jnp.where(seen, scores, -jnp.inf)
        top = jnp.max(scores, axis=-1, keepdims=True)
        weights = jnp.exp(scores - top)
        probs = (weights / jnp.sum(weights, axis=-1, keepdims=True)).astype(BF)
        out[:, part] = jnp.dot(probs, values, preferred_element_type=F32).astype(BF)


def attend_local(tokens, w_query, w_key, w_value):
    length, columns = tokens.shape[0], w_query.shape[1]
    return pl.pallas_call(
        attend_kernel,
        in_specs=[pl.BlockSpec(memory_space=pltpu.VMEM)] * 4,
        out_specs=pl.BlockSpec(memory_space=pltpu.VMEM),
        out_shape=jax.ShapeDtypeStruct((length, columns), BF),
        compiler_params=pltpu.CompilerParams(vmem_limit_bytes=48 * 1024 * 1024),
        cost_estimate=pl.CostEstimate(
            flops=4 * length * D * columns, bytes_accessed=2 * D * (length + 2 * columns), transcendentals=length * length * 2
        ),
    )(tokens, w_query, w_key, w_value)


def routing_table(routes, experts, capacity):
    number = routes.shape[0]
    same = routes[:, None] == routes[None, :]
    earlier = lax.broadcasted_iota(jnp.int32, (number, number), 1) < lax.broadcasted_iota(
        jnp.int32, (number, number), 0
    )
    slot = jnp.sum((same & earlier).astype(jnp.int32), axis=1)
    expert_hit = routes[None, :] == lax.broadcasted_iota(jnp.int32, (experts, number), 0)
    slot_hit = slot[None, :] == lax.broadcasted_iota(jnp.int32, (capacity, number), 0)
    return expert_hit[:, None, :] & slot_hit[None, :, :]


def gather_start(first, second, ring, pair):
    return shift(first, pair, 1), shift(second, ring, 1), shift(second, ring, -1)


def gather_middle(first, second, arrived):
    first_p, second_l, second_r = arrived
    half = second.shape[0] // 2
    return (
        rows_of(first, first_p, second_l[:half]),
        rows_of(first, first_p, second_r[half:]),
        rows_of(second, second_l, second_r),
    )


def gather_send(payload, ring, pair):
    return shift(payload[0], ring, 1), shift(payload[1], ring, -1), shift(payload[2], pair, 1)


def gather_last(arrived, n):
    left, right, _ = arrived
    return left[:n], right[n : 2 * n], rows_of(left[2 * n :], right[2 * n :])


def project_kernel(number, *refs):
    lhs, weights, out = refs[:number], refs[number : 2 * number], refs[2 * number]
    total = jnp.zeros(out.shape, F32)
    for left, right in zip(lhs, weights):
        total = total + jnp.dot(left[...], right[...], preferred_element_type=F32)
    out[...] = total.astype(BF)


def project(lhs, weights):
    rows, width = lhs[0].shape[0], weights[0].shape[1]
    tile = 512
    number = len(lhs)
    depth = sum(w.shape[0] for w in weights)
    return pl.pallas_call(
        functools.partial(project_kernel, number),
        grid=(width // tile,),
        in_specs=[pl.BlockSpec(v.shape, lambda j: (0, 0)) for v in lhs]
        + [pl.BlockSpec((w.shape[0], tile), lambda j: (0, j)) for w in weights],
        out_specs=pl.BlockSpec((rows, tile), lambda j: (0, j)),
        out_shape=jax.ShapeDtypeStruct((rows, width), BF),
        compiler_params=pltpu.CompilerParams(vmem_limit_bytes=60 * 1024 * 1024),
        cost_estimate=pl.CostEstimate(
            flops=2 * rows * width * depth, bytes_accessed=2 * depth * (rows + width), transcendentals=0
        ),
    )(*lhs, *weights)


OUT_TILES = 4
HIDDEN_TILE = 256


def ffn_kernel(rows, out_rows, *refs):
    number = len(rows)
    pieces = refs[:number]
    gates, ups, downs = refs[number : number + 2], refs[number + 2 : number + 4], refs[number + 4 : number + 6]
    outs = refs[number + 6 : number + 6 + len(out_rows)]
    x, wg, wu, wd, act, res, x_sem, g_sem, u_sem, d_sem, o_sem = refs[number + 6 + len(out_rows) :]
    hidden = gates[0].shape[0]

    x_copies, out_copies = [], []
    start = 0
    for i, count in enumerate(rows):
        part = pl.ds(start, count)
        x_copies.append(pltpu.make_async_copy(pieces[i], x.at[part], x_sem.at[i]))
        start += count
    start = 0
    for i, count in enumerate(out_rows):
        part = pl.ds(start, count)
        out_copies.append(pltpu.make_async_copy(res.at[part], outs[i], o_sem.at[i]))
        start += count
    g_copies, u_copies, d_copies = [], [], []
    for side in range(2):
        part = pl.ds(side * hidden, hidden)
        g_copies.append(pltpu.make_async_copy(gates[side], wg.at[part], g_sem.at[side]))
        u_copies.append(pltpu.make_async_copy(ups[side], wu.at[part], u_sem.at[side]))
        d_copies.append(pltpu.make_async_copy(downs[side], wd.at[part], d_sem.at[side]))
    for copy in x_copies:
        copy.start()
    for side in range(2):
        g_copies[side].start()
        u_copies[side].start()
    for copy in d_copies:
        copy.start()
    for copy in x_copies:
        copy.wait()
    contract = (((1,), (1,)), ((), ()))
    for side in range(2):
        g_copies[side].wait()
        u_copies[side].wait()
        for start in range(0, hidden, HIDDEN_TILE):
            part = pl.ds(side * hidden + start, min(HIDDEN_TILE, hidden - start))
            gate = lax.dot_general(x[...], wg[part, :], contract, preferred_element_type=F32)
            lifted = lax.dot_general(x[...], wu[part, :], contract, preferred_element_type=F32)
            act[:, part] = (gate / (1.0 + jnp.exp(-gate)) * lifted).astype(BF)
    for copy in d_copies:
        copy.wait()
    cols = D // OUT_TILES
    for j in range(OUT_TILES):
        part = pl.ds(j * cols, cols)
        res[:, part] = jnp.dot(act[...], wd[:, part], preferred_element_type=F32).astype(BF)
    for copy in out_copies:
        copy.start()
    for copy in out_copies:
        copy.wait()


def ffn(pieces, gates, ups, downs, out_rows=None):
    rows = tuple(p.shape[0] for p in pieces)
    out_rows = out_rows or rows
    total, number = sum(rows), len(rows)
    hidden = gates[0].shape[0]
    hbm_spec = pl.BlockSpec(memory_space=pltpu.HBM)
    return pl.pallas_call(
        functools.partial(ffn_kernel, rows, out_rows),
        in_specs=[hbm_spec] * (number + 6),
        out_specs=[hbm_spec] * len(out_rows),
        out_shape=[jax.ShapeDtypeStruct((count, D), BF) for count in out_rows],
        scratch_shapes=[
            pltpu.VMEM((total, D), BF),
            pltpu.VMEM((2 * hidden, D), BF),
            pltpu.VMEM((2 * hidden, D), BF),
            pltpu.VMEM((2 * hidden, D), BF),
            pltpu.VMEM((total, 2 * hidden), BF),
            pltpu.VMEM((total, D), BF),
            pltpu.SemaphoreType.DMA((number,)),
            pltpu.SemaphoreType.DMA((2,)),
            pltpu.SemaphoreType.DMA((2,)),
            pltpu.SemaphoreType.DMA((2,)),
            pltpu.SemaphoreType.DMA((len(out_rows),)),
        ],
        compiler_params=pltpu.CompilerParams(vmem_limit_bytes=60 * 1024 * 1024),
        cost_estimate=pl.CostEstimate(
            flops=12 * total * hidden * D, bytes_accessed=12 * hidden * D + 4 * total * D, transcendentals=2 * total * hidden
        ),
    )(*pieces, *gates, *ups, *downs)


def after(values, *others):
    return lax.optimization_barrier((values, others))[0]


def per_device(
    tokens, w_query, w_key, w_value, w_out, w_gate, w_up, w_down, route, old_out, cotangent
):
    experts = 8
    capacity = 2
    length = tokens.shape[0]
    blocks = length // BLOCK
    piece_rows = BLOCK // experts
    old_count = experts - max(1, experts // 4)
    yl, z, core = lax.axis_index("yl"), lax.axis_index("z"), lax.axis_index("core")
    own = yl * 4 + z

    width = D // 2
    own_out = lax.dynamic_slice_in_dim(w_out, core * width, width, 1)
    wa, wb = own_out[:HEAD_DIM], own_out[HEAD_DIM:]
    w1 = gather_start(wa, wb, "z", "yl")
    gates = [w_gate[0], shift(w_gate[0], "core", 1)]

    routes = route[:, 0]
    hits = routing_table(routes, experts, capacity)
    table = hits.astype(BF)
    places = jnp.sum(
        hits.astype(jnp.int32) * lax.broadcasted_iota(jnp.int32, hits.shape, 2), axis=2
    )
    mine = lax.dynamic_slice_in_dim(places, own, 1, 0)[0]
    own_tokens = [
        lax.dynamic_slice_in_dim(tokens, mine[slot] * BLOCK, BLOCK, 0) for slot in range(capacity)
    ]

    heads_out = attend_local(tokens, w_query, w_key, w_value)
    outgoing = jnp.einsum(
        "jcb,brd->jcrd", table, heads_out.reshape(blocks, BLOCK, -1), preferred_element_type=F32
    ).astype(BF)
    heads_in = lax.all_to_all(
        outgoing.reshape(experts, capacity * BLOCK, -1), ("yl", "z"), split_axis=0, concat_axis=0, tiled=True
    )
    payload, heads_in = after((gather_middle(wa, wb, w1), heads_in), gates[1])
    w2 = gather_send(payload, "z", "yl")
    heads_in = rows_of_cores(heads_in)

    def near(dy, dz):
        at = ((yl + dy) % 2) * 4 + (z + dz) % 4
        return lax.dynamic_slice_in_dim(heads_in, at, 1, 0)[0]

    hd = {(dy, dz): near(dy, dz) for dy in range(2) for dz in (0, -1, 1, 2)}

    def a(dy, dz):
        return hd[dy, dz][:, :HEAD_DIM]

    def b(dy, dz):
        return hd[dy, dz][:, HEAD_DIM:]

    half = HEAD_DIM // 2
    lhs = [
        hd[0, 0],
        a(1, 0),
        b(0, -1),
        b(0, 1),
        jnp.concatenate([a(0, -1), a(1, -1), b(0, 2)[:, :half]], axis=1),
        jnp.concatenate([a(0, 1), a(1, 1), b(0, 2)[:, half:]], axis=1),
        jnp.concatenate([b(1, 0), b(1, -1), b(1, 1)], axis=1),
        a(0, 2),
        a(1, 2),
        b(1, 2),
    ]
    w2, lhs = after((w2, lhs))
    last = gather_last(w2, HEAD_DIM)
    w3 = gather_send(last, "z", "yl")
    ups = [w_up[0], shift(after(w_up[0], last), "core", 1)]
    terms = lax.dot_general(
        after(cotangent, last), heads_out, (((0,), (0,)), ((), ())), preferred_element_type=F32
    ).astype(BF)
    w3, lhs, terms = after((w3, lhs, terms.reshape(8, 2, D // 16, -1)), ups[1])
    attention = project(lhs, [own_out, *w1, *w2, *w3])
    rows = capacity * BLOCK
    here = attention[:rows]
    there = shift(attention[rows:], "core", 1)
    first_half = jnp.where(core == 0, here, there)
    second_half = jnp.where(core == 0, there, here)
    both = jnp.concatenate([first_half, second_half], axis=1)
    ha = plus(own_tokens[0], both[:BLOCK])
    hb = plus(own_tokens[1], both[BLOCK:])

    downs = [w_down[0], shift(after(w_down[0], w3), "core", 1)]
    r1 = gather_start(ha, hb, "x", "yh")
    kept, given = halves(terms, 1, core)
    pairs = plus(kept, shift(given, "core", 1)).reshape(4, 2, D // 16, -1)
    first, pairs = after((gather_middle(ha, hb, r1), pairs), downs[1])
    r2 = gather_send(first, "x", "yh")
    pa, pb, p_ap, p_bl, p_br = early = ffn([ha, hb, *r1], gates, ups, downs)
    last, left_right, pairs = after((gather_last(r2, BLOCK), list(r2[:2]), pairs), early)
    r3 = gather_send(last, "x", "yh")
    kept, given = halves(pairs, 1, lax.axis_index("yh"))
    quads = plus(kept, shift(given, "yh", 1))
    x = lax.axis_index("x")
    term = [lax.dynamic_slice_in_dim(quads, (x + k) % 4, 1, 0)[0] for k in range(4)]
    middle = ffn(left_right, gates, ups, downs)
    late, (p_left, p_right), term = after(([r2[2], *r3], middle, term))
    p_middle, p_sides, p_aa, p_apa, p_bpa = ffn(late, gates, ups, downs, (BLOCK, 2 * BLOCK, BLOCK, BLOCK, BLOCK))

    n, h = BLOCK, BLOCK // 2
    s_aa = shift(p_aa, "x", -1)
    s_apa = shift(p_apa, "x", 1)
    s_bpa = shift(p_bpa, "yh", 1)
    left = rows_of(plus(p_left[:n], s_aa), p_left[n : 2 * n], plus(p_left[2 * n :], s_bpa[:h]))
    right = rows_of(p_right[:n], plus(p_right[n : 2 * n], s_apa), plus(p_right[2 * n :], s_bpa[h:]))
    s_left = shift(left, "x", -1)
    s_right = shift(right, "x", 1)
    s_sides = shift(p_sides, "yh", 1)
    s_middle = shift(after(p_middle, s_bpa), "yh", 1)
    t_ap = plus(p_ap, s_left[n : 2 * n], s_right[n : 2 * n])
    t_bl = rows_of(plus(p_bl[:h], s_sides[:h], s_left[2 * n :]), plus(p_bl[h:], s_sides[h:n]))
    t_br = rows_of(plus(p_br[:h], s_sides[n : n + h]), plus(p_br[h:], s_sides[n + h :], s_right[2 * n :]))
    e_a = shift(t_ap, "yh", 1)
    e_bl = shift(t_bl, "x", -1)
    e_br = shift(t_br, "x", 1)
    out_a = plus(pa, s_left[:n], s_right[:n], e_a)
    out_b = plus(pb, s_middle, e_bl, e_br)

    done = rows_of(plus(ha, out_a), plus(hb, out_b)).reshape(capacity, experts, piece_rows, D)
    done, term = after((done, term))
    met = [shift(term[k], "x", k) for k in range(1, 4)]
    gradient = term[0].astype(F32) + met[0].astype(F32) + met[1].astype(F32) + met[2].astype(F32)
    returned = lax.all_to_all(
        jnp.moveaxis(done, 1, 0), ("yl", "z"), split_axis=0, concat_axis=0, tiled=True
    )
    joined = jnp.einsum("jcb,jcrd->brd", table, returned, preferred_element_type=F32)
    fresh = (routes >= old_count).astype(F32)
    gap = joined - old_out.astype(F32)
    divergence = 0.5 * jnp.mean(gap * gap, axis=-1) * fresh[:, None]

    return (joined.astype(BF), divergence, gradient)


def halves(value, axis, index):
    return (
        jnp.squeeze(lax.dynamic_slice_in_dim(value, index, 1, axis), axis),
        jnp.squeeze(lax.dynamic_slice_in_dim(value, 1 - index, 1, axis), axis),
    )


def rows_of_cores(heads_in):
    return jnp.concatenate([heads_in, shift(heads_in, "core", 1)], axis=1)


def solution(mesh):
    fine = Mesh(mesh.devices.reshape(tuple(SIZES.values())), AXES)
    replica, expert = ("x", "yh", "core"), ("yl", "z")
    return jax.shard_map(
        per_device,
        mesh=fine,
        in_specs=(
            P(replica, None),
            P(None, expert),
            P(None, expert),
            P(None, expert),
            P(expert, None),
            P(expert, replica, None),
            P(expert, replica, None),
            P(expert, replica, None),
            P(replica, None),
            P(replica, expert, None),
            P(replica, None),
        ),
        out_specs=(
            P(replica, expert, None),
            P(replica, expert),
            P(replica, expert),
        ),
        check_vma=False,
    )
```
